256 devices in a mesh: lat: 16 (over x_hi, y, core), lon: 16 (over x_lo, z).
Axes of the slice: x: 4 (x_hi: 2, x_lo: 2; x = x_hi * 2 + x_lo), y: 4, z: 8, core: 2. Of those that a mesh axis runs over, the one named last changes fastest.
Arguments:
- queries: bfloat16 [16, 32, 64, 1024], P('lat', 'lon'), may hold values from -36 to 36
- keys_values: bfloat16 [2, 16, 32, 64, 1024], P(None, 'lat', 'lon'), may hold values from -4 to 4
- cotangent: bfloat16 [16, 32, 64, 1024], P('lat', 'lon'), may hold values from -6 to 6
- blocks: int32 [16, 32, 6], P('lat', 'lon'), may hold values from 0 to 511, as said below
Outputs:
- attended: bfloat16 [16, 32, 64, 1024], P('lat', 'lon')
- grad_queries: bfloat16 [16, 32, 64, 1024], P('lat', 'lon')
- grad_keys_values: bfloat16 [2, 16, 32, 64, 1024], P(None, 'lat', 'lon')
The draws below stay inside these ranges and needn't reach their ends.
Inputs may be any that keep to these rules, and one draw needn't show every extreme that they name: Entry 0 of each query block's list is the block itself. The other 5 entries are distinct blocks other than itself, whose band differs by at most one from the query block's band and whose sector differs by at most one, counted cyclically over 32 sectors.
All inputs are finite; a program needn't handle non-finite values.
Results may differ from the reference program's by a relative error of at most 0.0085.
Values may be sent and summed in bfloat16 or wider, within the bound.
A program may use at most 128 MiB of HBM per device.

```python
import jax
import jax.numpy as jnp
from jax import lax

HEADS = 16
HEAD_DIM = 64
D = 1024
CELLS = 64
SAMPLES = 6
GLAT = 16
GLON = 32


def key_field(key):
    base = jax.random.fold_in(key, 11)
    return jnp.clip(jax.random.normal(base, (GLAT, GLON, CELLS, D), jnp.float32), -4.0, 4.0)


def draw_keys_values(key, part):
    keys = key_field(key)
    other = jax.random.fold_in(key, 12)
    values = jnp.clip(jax.random.normal(other, (GLAT, GLON, CELLS, D), jnp.float32), -4.0, 4.0)
    return jnp.stack([keys, values]).astype(jnp.bfloat16)


def draw_queries(key, part):
    other = jax.random.fold_in(key, 13)
    queries = jnp.clip(jax.random.normal(other, (GLAT, GLON, CELLS, D), jnp.float32), -4.0, 4.0)
    return queries.astype(jnp.bfloat16)


def draw_blocks(key, part):
    band_ids = jnp.arange(GLAT, dtype=jnp.int32).reshape(GLAT, 1, 1)
    sector_ids = jnp.arange(GLON, dtype=jnp.int32).reshape(1, GLON, 1)
    shifts = jnp.arange(9, dtype=jnp.int32)
    target_band = band_ids + shifts // 3 - 1
    target_sector = (sector_ids + shifts % 3 - 1) % GLON
    noise = jax.random.randint(key, (GLAT, GLON, 9), 0, 1 << 20)
    invalid = (target_band < 0) | (target_band >= GLAT) | (shifts == 4)
    ranking = noise * 16 + shifts + jnp.where(invalid, 1 << 26, 0)
    picked = jnp.argsort(ranking, axis=-1, stable=True)[:, :, :SAMPLES - 1]
    targets = target_band * GLON + target_sector
    chosen = jnp.take_along_axis(targets, picked, axis=-1)
    itself = jnp.broadcast_to(band_ids * GLON + sector_ids, (GLAT, GLON, 1))
    return jnp.concatenate([itself, chosen], axis=-1).astype(jnp.int32)


def levels(key, shape, cuts, low, top_value):
    def one(axis_at, shards_of):
        heights = jax.random.uniform(jax.random.fold_in(jax.random.fold_in(key, 6), axis_at), (shards_of,), jnp.float32, low / len(cuts), top_value / len(cuts))
        return jnp.repeat(jnp.exp(heights), shape[axis_at] // shards_of).reshape((-1,) + (1,) * (len(shape) - axis_at - 1))

    gain = one(*cuts[0])
    for cut in cuts[1:]:
        gain = gain * one(*cut)
    return gain


def bell_draw(own_key, extent, scale, bound, pieces=(), kind=jnp.bfloat16):
    array = jax.random.normal(own_key, extent, jnp.float32) * scale
    if len(pieces) > 0:
        array = levels(own_key, extent, pieces, -0.22, 0.18) * array
    return jnp.clip(array, min=-bound, max=bound).astype(kind)


def setup_inputs(seed: int = 0) -> dict:
    seeds = jax.random.split(jax.random.key(seed), 5)
    queries = draw_queries(jax.random.fold_in(seeds[4], 71), 0)
    keys_values = draw_keys_values(jax.random.fold_in(seeds[4], 71), 0)
    cotangent = bell_draw(seeds[2], (GLAT, GLON, CELLS, D), 1.0, 6.0, ((0, 16), (1, 16)))
    blocks = draw_blocks(jax.random.fold_in(seeds[4], 71), 0)
    return dict(queries=queries, keys_values=keys_values, cotangent=cotangent, blocks=blocks)


def attend(query, key_sel, value_sel, upstream):
    scale = HEAD_DIM ** -0.5
    query_heads = query.astype(jnp.float32).reshape(CELLS, HEADS, HEAD_DIM)
    key_heads = key_sel.astype(jnp.float32).reshape(SAMPLES * CELLS, HEADS, HEAD_DIM)
    value_heads = value_sel.astype(jnp.float32).reshape(SAMPLES * CELLS, HEADS, HEAD_DIM)
    upstream_heads = upstream.astype(jnp.float32).reshape(CELLS, HEADS, HEAD_DIM)
    scores = jnp.einsum("ihe,jhe->hij", query_heads, key_heads) * scale
    highest = jnp.max(scores, axis=2, keepdims=True)
    raised = jnp.exp(scores - highest)
    weights = raised / jnp.sum(raised, axis=2, keepdims=True)
    weights_low = weights.astype(jnp.bfloat16)
    attended = jnp.einsum("hij,jhe->ihe", weights_low.astype(jnp.float32), value_heads)
    attended = attended.reshape(CELLS, D).astype(jnp.bfloat16)
    pressure = jnp.einsum("ihe,jhe->hij", upstream_heads, value_heads)
    inner = jnp.sum(weights * pressure, axis=2, keepdims=True)
    score_grad = (weights * (pressure - inner) * scale).astype(jnp.bfloat16)
    grad_query = jnp.einsum("hij,jhe->ihe", score_grad.astype(jnp.float32), key_heads)
    grad_query = grad_query.reshape(CELLS, D).astype(jnp.bfloat16)
    grad_key = jnp.einsum("hij,ihe->jhe", score_grad.astype(jnp.float32), query_heads).reshape(SAMPLES, CELLS, D)
    grad_value = jnp.einsum("hij,ihe->jhe", weights_low.astype(jnp.float32), upstream_heads).reshape(SAMPLES, CELLS, D)
    return attended, grad_query, grad_key, grad_value


def reference(queries, keys_values, cotangent, blocks):
    count = GLAT * GLON
    query_flat = queries.reshape(count, CELLS, D)
    key_flat = keys_values[0].reshape(count, CELLS, D)
    value_flat = keys_values[1].reshape(count, CELLS, D)
    upstream_flat = cotangent.reshape(count, CELLS, D)
    list_flat = blocks.reshape(count, SAMPLES).astype(jnp.int32)

    def step(carry, item):
        query, upstream, chosen = item
        attended, grad_query, grad_key, grad_value = attend(query, key_flat[chosen], value_flat[chosen], upstream)
        carry = carry.at[0, chosen].add(grad_key)
        carry = carry.at[1, chosen].add(grad_value)
        return carry, (attended, grad_query)

    zeros = jnp.zeros((2, count, CELLS, D), jnp.float32)
    grads, outputs = lax.scan(step, zeros, (query_flat, upstream_flat, list_flat))
    attended = outputs[0].reshape(GLAT, GLON, CELLS, D)
    grad_queries = outputs[1].reshape(GLAT, GLON, CELLS, D)
    grad_keys_values = grads.reshape(2, GLAT, GLON, CELLS, D).astype(jnp.bfloat16)
    return (attended, grad_queries, grad_keys_values)
```

```python
import jax
import jax.numpy as jnp
from jax import lax
from jax.experimental import pallas as pl
from jax.experimental.pallas import tpu as pltpu
from jax.sharding import PartitionSpec as P

HEAD_DIM = 64
CELLS = 64
D = 1024
CH = 256
NC = D // CH
PER = CH // HEAD_DIM
SECTORS = 2
SAMPLES = 6
OUTER, OWN, INNER = 0, 1, 2
HIDE = -1e30


def dot(a, b, ca, cb):
    return lax.dot_general(a, b, (((ca,), (cb,)), ((), ())), preferred_element_type=jnp.float32)


def make_kernel(n_lat, n_lon):
    sector_total = n_lon * SECTORS

    def kernel(
        blocks, q_hbm, kv_hbm, do_hbm, att_hbm, gq_hbm, gkv_hbm,
        ext, qs, dos, att_s, gq_s, gkv_s, g_own, g_out, g_halo,
        s_ic, s_oc, s_in, s_out, s_halo, r_ic, r_oc, r_in, r_out, r_halo,
        send_sem, recv_sem, load_sem, store_sem,
    ):
        i = lax.axis_index("lat")
        j = lax.axis_index("lon")
        core = lax.rem(i, 2)
        partner = i + 1 - 2 * core
        outer = lax.rem(i + 2 * core - 1 + n_lat, n_lat)
        left = lax.rem(j + n_lon - 1, n_lon)
        right = lax.rem(j + 1, n_lon)

        def cols(t):
            return pl.ds(pl.multiple_of(t * CH, CH), CH)

        def loads(t):
            return [
                pltpu.make_async_copy(kv_hbm.at[:, 0, :, :, cols(t)], ext.at[t, :, OWN, 1:3], load_sem.at[t, 0]),
                pltpu.make_async_copy(q_hbm.at[0, :, :, cols(t)], qs.at[t], load_sem.at[t, 1]),
                pltpu.make_async_copy(do_hbm.at[0, :, :, cols(t)], dos.at[t], load_sem.at[t, 2]),
            ]

        def stores(t):
            return [
                pltpu.make_async_copy(att_s.at[t], att_hbm.at[0, :, :, cols(t)], store_sem.at[t, 0]),
                pltpu.make_async_copy(gq_s.at[t], gq_hbm.at[0, :, :, cols(t)], store_sem.at[t, 1]),
                pltpu.make_async_copy(gkv_s.at[t], gkv_hbm.at[:, 0, :, :, cols(t)], store_sem.at[t, 2]),
            ]

        def remote(t, kind, src, dst, device):
            return pltpu.make_async_remote_copy(
                src_ref=src, dst_ref=dst, send_sem=send_sem.at[t, kind], recv_sem=recv_sem.at[t, kind],
                device_id=device, device_id_type=pl.DeviceIdType.MESH,
            )

        def to_lat(where):
            return (where, j)

        def to_lon(where):
            return (i, where)

        def first(t):
            return [
                remote(t, 0, kv_hbm.at[:, 0, :, :, cols(t)], ext.at[t, :, OUTER, 1:3], to_lat(outer)),
                remote(t, 1, kv_hbm.at[:, 0, 0, :, cols(t)], ext.at[t, :, OWN, 3], to_lon(left)),
                remote(t, 2, kv_hbm.at[:, 0, 1, :, cols(t)], ext.at[t, :, OWN, 0], to_lon(right)),
                remote(t, 3, kv_hbm.at[:, 0, :, :, cols(t)], ext.at[t, :, INNER, 1:3], to_lat(partner)),
            ]

        def second(t):
            return [
                remote(t, 4, ext.at[t, :, OUTER, 1], ext.at[t, :, OUTER, 3], to_lon(left)),
                remote(t, 5, ext.at[t, :, OUTER, 2], ext.at[t, :, OUTER, 0], to_lon(right)),
                remote(t, 6, ext.at[t, :, OWN, 3], ext.at[t, :, INNER, 3], to_lat(partner)),
                remote(t, 7, ext.at[t, :, OWN, 0], ext.at[t, :, INNER, 0], to_lat(partner)),
            ]

        def third(t):
            return [
                remote(t, 8, s_oc.at[t, 0], r_oc.at[t, 0], to_lon(left)),
                remote(t, 9, s_oc.at[t, 1], r_oc.at[t, 1], to_lon(right)),
                remote(t, 10, s_ic.at[t], r_ic.at[t], to_lat(partner)),
                remote(t, 11, s_in.at[t], r_in.at[t], to_lat(partner)),
            ]

        def fourth(t):
            return [
                remote(t, 12, s_out.at[t], r_out.at[t], to_lat(outer)),
                remote(t, 13, s_halo.at[t, 0], r_halo.at[t, 0], to_lon(left)),
                remote(t, 14, s_halo.at[t, 1], r_halo.at[t, 1], to_lon(right)),
            ]

        def start(copies):
            for copy in copies:
                copy.start()

        def forward(t):
            a, from_right, from_left, _ = first(t)
            to_left, to_right, right_in, left_in = second(t)
            from_right.wait_recv()
            right_in.start()
            from_left.wait_recv()
            left_in.start()
            a.wait_recv()
            to_left.start()
            to_right.start()

        sign = 1 - 2 * core
        bias = []
        for b in range(SECTORS):
            codes = []
            for s in range(SAMPLES):
                block = blocks[0, b, s]
                band = block // sector_total
                sector = block % sector_total
                column = (sector - (SECTORS * j + b) + 1 + sector_total) % sector_total
                codes.append((1 + sign * (band - i)) * 3 + column)
            row = []
            for o in range(9):
                listed = codes[0] == o
                for code in codes[1:]:
                    listed = listed | (code == o)
                row.append(jnp.where(listed, 0.0, HIDE).astype(jnp.float32))
            bias.append(row)

        head = lax.broadcasted_iota(jnp.int32, (CELLS, CH), 1) // HEAD_DIM
        on = [jnp.where(head == h, 1.0, 0.0).astype(jnp.float32) for h in range(PER)]
        on_low = [o.astype(jnp.bfloat16) for o in on]

        def spread(x):
            return jnp.concatenate([x * m for m in on_low], axis=0)

        def gathered(x):
            total = x[0:CELLS] * on[0]
            for h in range(1, PER):
                total = total + x[h * CELLS : (h + 1) * CELLS] * on[h]
            return total

        def compute(t):
            scale = HEAD_DIM ** -0.5
            grads = ([], [])
            for b in range(SECTORS):
                qbd = spread(qs[t, b])
                dbd = spread(dos[t, b])
                keys = ext[t, 0, :, b : b + 3].reshape(9 * CELLS, CH)
                values = ext[t, 1, :, b : b + 3].reshape(9 * CELLS, CH)
                scores = dot(keys, qbd, 1, 1)
                scores = jnp.concatenate(
                    [scores[o * CELLS : (o + 1) * CELLS] + bias[b][o] for o in range(9)], axis=0
                )
                highest = jnp.max(scores, axis=0, keepdims=True)
                raised = jnp.exp((scores - highest) * scale)
                weights = raised * (1.0 / jnp.sum(raised, axis=0, keepdims=True))
                low = weights.astype(jnp.bfloat16)
                pressure = dot(values, dbd, 1, 1)
                inner = jnp.sum(weights * pressure, axis=0, keepdims=True)
                score_grad = (weights * (pressure - inner) * scale).astype(jnp.bfloat16)
                att_s[t, b] = gathered(dot(low, values, 0, 0)).astype(jnp.bfloat16)
                gq_s[t, b] = gathered(dot(score_grad, keys, 0, 0)).astype(jnp.bfloat16)
                grads[0].append(dot(score_grad, qbd, 1, 0).reshape(3, 3, CELLS, CH))
                grads[1].append(dot(low, dbd, 1, 0).reshape(3, 3, CELLS, CH))
            for kv in range(2):
                g0, g1 = grads[kv]
                middle = [[g0[r, 1] + g1[r, 0], g0[r, 2] + g1[r, 1]] for r in range(3)]
                edges = [[g0[r, 0], g1[r, 2]] for r in range(3)]
                for side in range(2):
                    s_oc[t, side, kv] = edges[OUTER][side].astype(jnp.bfloat16)
                    s_ic[t, side, kv] = edges[INNER][side].astype(jnp.bfloat16)
                    s_in[t, kv, side] = middle[INNER][side].astype(jnp.bfloat16)
                    g_halo[t, side, kv] = edges[OWN][side]
                    g_out[t, kv, side] = middle[OUTER][side]
                    g_own[t, kv, side] = middle[OWN][side]

        def middle(t):
            copies = third(t)
            out, to_left, to_right = fourth(t)
            copies[2].wait_recv()
            for side in range(2):
                s_halo[t, side] = (g_halo[t, side] + r_ic[t, side].astype(jnp.float32)).astype(jnp.bfloat16)
            to_left.start()
            to_right.start()
            copies[0].wait_recv()
            copies[1].wait_recv()
            for side in range(2):
                s_out[t, :, side] = (g_out[t, :, side] + r_oc[t, 1 - side].astype(jnp.float32)).astype(jnp.bfloat16)
            out.start()

        def finish(t):
            third(t)[3].wait_recv()
            for copy in fourth(t):
                copy.wait_recv()
            for side in range(2):
                total = (
                    g_own[t, :, side]
                    + r_in[t, :, side].astype(jnp.float32)
                    + r_out[t, :, side].astype(jnp.float32)
                    + r_halo[t, 1 - side].astype(jnp.float32)
                )
                gkv_s[t, :, side] = total.astype(jnp.bfloat16)
            stores(t)[2].start()

        for t in range(NC):
            start(loads(t))
        barrier = pltpu.get_barrier_semaphore()
        for device in (to_lat(outer), to_lat(partner), to_lon(left), to_lon(right)):
            pl.semaphore_signal(barrier, inc=1, device_id=device, device_id_type=pl.DeviceIdType.MESH)
        pl.semaphore_wait(barrier, 4)
        start(first(0))
        start(first(1))
        forward(0)
        start(first(2))

        @pl.loop(0, NC)
        def _(t):
            @pl.when(t + 1 < NC)
            def _():
                forward(t + 1)

            @pl.when(t + 3 < NC)
            def _():
                start(first(t + 3))

            for copy in loads(t):
                copy.wait()
            first(t)[3].wait_recv()
            for copy in second(t):
                copy.wait_recv()
            compute(t)
            start(third(t))
            for copy in stores(t)[:2]:
                copy.start()

            @pl.when(t >= 1)
            def _():
                middle(t - 1)

            @pl.when(t >= 2)
            def _():
                finish(t - 2)

        middle(NC - 1)
        finish(NC - 2)
        finish(NC - 1)

        @pl.loop(0, NC)
        def _(t):
            for copies in (first(t), second(t), third(t), fourth(t)):
                for copy in copies:
                    copy.wait_send()
            for copy in stores(t):
                copy.wait()

    return kernel


def solution(mesh):
    kernel = make_kernel(mesh.shape["lat"], mesh.shape["lon"])
    low, full = jnp.bfloat16, jnp.float32
    pair = (NC, 2, CELLS, CH)
    quad = (NC, 2, 2, CELLS, CH)

    def body(queries, keys_values, cotangent, blocks):
        anywhere = pl.BlockSpec(memory_space=pl.ANY)
        return pl.pallas_call(
            kernel,
            out_shape=(
                jax.ShapeDtypeStruct(queries.shape, low),
                jax.ShapeDtypeStruct(queries.shape, low),
                jax.ShapeDtypeStruct(keys_values.shape, low),
            ),
            in_specs=[pl.BlockSpec(memory_space=pltpu.SMEM), anywhere, anywhere, anywhere],
            out_specs=(anywhere, anywhere, anywhere),
            scratch_shapes=[
                pltpu.VMEM((NC, 2, 3, SECTORS + 2, CELLS, CH), low),
                *[pltpu.VMEM(pair, low)] * 4,
                pltpu.VMEM(quad, low),
                *[pltpu.VMEM(quad, full)] * 3,
                *[pltpu.VMEM(quad, low)] * 10,
                pltpu.SemaphoreType.DMA((NC, 15)),
                pltpu.SemaphoreType.DMA((NC, 15)),
                pltpu.SemaphoreType.DMA((NC, 3)),
                pltpu.SemaphoreType.DMA((NC, 3)),
            ],
            compiler_params=pltpu.CompilerParams(
                collective_id=0, has_side_effects=True, vmem_limit_bytes=50 * 1024 * 1024
            ),
            cost_estimate=pl.CostEstimate(flops=4_000_000_000, bytes_accessed=4_000_000, transcendentals=1_200_000),
        )(blocks, queries, keys_values, cotangent)

    placed = (
        P("lat", "lon", None, None),
        P(None, "lat", "lon", None, None),
        P("lat", "lon", None, None),
        P("lat", "lon", None),
    )
    return jax.shard_map(
        body,
        mesh=mesh,
        in_specs=placed,
        out_specs=(placed[0], placed[0], placed[1]),
        check_vma=False,
    )
```

```python
import jax
import jax.numpy as jnp
from jax import lax
from jax.experimental import pallas as pl
from jax.experimental.pallas import tpu as pltpu
from jax.sharding import PartitionSpec as P

HEAD_DIM = 64
CELLS = 64
D = 1024
CH = 256
STEPS = D // CH
PER = CH // HEAD_DIM
NC = 2
N = STEPS // NC
SECTORS = 2
SAMPLES = 6
OUTER, OWN, INNER = 0, 1, 2
SEEN = ((0, 2, 3), (2, 3, 1))
HIDE = -1e30


def dot(a, b, ca, cb):
    return lax.dot_general(a, b, (((ca,), (cb,)), ((), ())), preferred_element_type=jnp.float32)


def make_kernel(n_lat, n_lon):
    sector_total = n_lon * SECTORS

    def kernel(
        blocks, q_hbm, kv_hbm, do_hbm, att_hbm, gq_hbm, gkv_hbm,
        ext, qs, dos, att_s, gq_s, gkv_s, g_own, g_out, g_halo,
        s_oc, s_in, s_out, s_halo, r_oc, r_yc, r_in, r_out, r_halo,
        send_sem, recv_sem, load_sem, store_sem,
    ):
        i = lax.axis_index("lat")
        j = lax.axis_index("lon")
        core = lax.rem(i, 2)
        partner = i + 1 - 2 * core
        half = n_lat // 2
        edge = (i == 0) | (i == n_lat - 1)
        seam = (i == half - 1) | (i == half)
        inside = jnp.logical_not(edge)
        plain = inside & jnp.logical_not(seam)
        beside = plain & (i >= half - 3) & (i <= half + 2)
        by_lon = (inside & jnp.logical_not(beside), seam)
        by_lat = (beside, plain)
        outer = jnp.where(edge, partner, i + 2 * core - 1)
        values_to = jnp.where(i == half - 1, 0, jnp.where(i == half, n_lat - 1, outer))
        values_to = jnp.where(i == 0, half, jnp.where(i == n_lat - 1, half - 1, values_to))
        values_from = jnp.where(i == half - 1, n_lat - 1, jnp.where(i == half, 0, outer))
        values_from = jnp.where(i == 0, half - 1, jnp.where(i == n_lat - 1, half, values_from))
        left = lax.rem(j + n_lon - 1, n_lon)
        right = lax.rem(j + 1, n_lon)

        def cols(u):
            return pl.ds(u * CH, CH)

        def loads(u):
            return [
                pltpu.make_async_copy(kv_hbm.at[0, 0, :, :, cols(u)], ext.at[u // N, OWN, 2:4, 0, u % N], load_sem.at[u, 0]),
                pltpu.make_async_copy(kv_hbm.at[1, 0, :, :, cols(u)], ext.at[u // N, OWN, 2:4, 1, u % N], load_sem.at[u, 1]),
                pltpu.make_async_copy(q_hbm.at[0, :, :, cols(u)], qs.at[u], load_sem.at[u, 2]),
                pltpu.make_async_copy(do_hbm.at[0, :, :, cols(u)], dos.at[u], load_sem.at[u, 3]),
            ]

        def stores(u):
            return [
                pltpu.make_async_copy(att_s.at[u], att_hbm.at[0, :, :, cols(u)], store_sem.at[u, 0]),
                pltpu.make_async_copy(gq_s.at[u], gq_hbm.at[0, :, :, cols(u)], store_sem.at[u, 1]),
                pltpu.make_async_copy(gkv_s.at[u, :, 0], gkv_hbm.at[0, 0, :, :, cols(u)], store_sem.at[u, 2]),
                pltpu.make_async_copy(gkv_s.at[u, :, 1], gkv_hbm.at[1, 0, :, :, cols(u)], store_sem.at[u, 3]),
            ]

        def remote(t, kind, src, dst, device, when=None):
            def make():
                return pltpu.make_async_remote_copy(
                    src_ref=src, dst_ref=dst, send_sem=send_sem.at[t, kind], recv_sem=recv_sem.at[t, kind],
                    device_id=device, device_id_type=pl.DeviceIdType.MESH,
                )

            return when, make

        def to_lat(where):
            return (where, j)

        def to_lon(where):
            return (i, where)

        def owners(t, kind, src, dst):
            return {
                "o": remote(t, kind, src, dst, to_lat(outer), plain),
                "ok": remote(t, kind, src.at[:, 0], dst.at[:, 0], to_lat(outer), seam),
                "ov": remote(t, kind + 1, src.at[:, 1], dst.at[:, 1], to_lat(values_to), seam),
                "relay": remote(t, kind + 1, dst.at[:, 1], dst.at[:, 1], to_lat(values_to), edge),
            }

        def first(t):
            own = ext.at[t, OWN]
            return {
                **owners(t, 0, own.at[2:4], ext.at[t, OUTER, 2:4]),
                "left": remote(t, 2, own.at[2], own.at[1], to_lon(left)),
                "right": remote(t, 3, own.at[3], own.at[0], to_lon(right)),
                "in": remote(t, 4, own.at[2:4], ext.at[t, INNER, 2:4], to_lat(partner)),
            }

        def second(t):
            near, far, across = ext.at[t, OWN], ext.at[t, OUTER], ext.at[t, INNER]
            found = {"in": remote(t, 5, near.at[0:2], across.at[0:2], to_lat(partner))}
            for kv in range(2):
                found["left", kv] = remote(t, 6 + kv, far.at[2, kv], far.at[1, kv], to_lon(left), by_lon[kv])
                found["right", kv] = remote(t, 8 + kv, far.at[3, kv], far.at[0, kv], to_lon(right), by_lon[kv])
                found["out", kv] = remote(t, 10 + kv, near.at[0:2, kv], far.at[0:2, kv], to_lat(outer), by_lat[kv])
            return found

        def third(t):
            found = {"in": remote(t, 12, s_in.at[t], r_in.at[t], to_lat(partner))}
            for kv in range(2):
                found["left", kv] = remote(t, 13 + kv, s_oc.at[t, 0, kv], r_oc.at[t, 0, kv], to_lon(left), by_lon[kv])
                found["right", kv] = remote(t, 15 + kv, s_oc.at[t, 1, kv], r_oc.at[t, 1, kv], to_lon(right), by_lon[kv])
                found["out", kv] = remote(t, 17 + kv, s_oc.at[t, :, kv], r_yc.at[t, :, kv], to_lat(outer), by_lat[kv])
            return found

        def fourth(t):
            return {
                **owners(t, 19, s_out.at[t], r_out.at[t]),
                "left": remote(t, 21, s_halo.at[t, 0], r_halo.at[t, 0], to_lon(left)),
                "right": remote(t, 22, s_halo.at[t, 1], r_halo.at[t, 1], to_lon(right)),
            }

        def each(make, t, names, act):
            copies = [make(t)[name] for name in names]
            while copies:
                when = copies[0][0]
                same = [copy for copy in copies if copy[0] is when]
                copies = [copy for copy in copies if copy[0] is not when]

                def run():
                    for _, copy in same:
                        act(copy())

                if when is None:
                    run()
                else:
                    pl.when(when)(run)

        def start(make, t, names):
            each(make, t, names, lambda copy: copy.start())

        def arrived(make, t, names):
            each(make, t, names, lambda copy: copy.wait_recv())

        def arrived_values(make, t):
            @pl.when(jnp.logical_not(plain))
            def _():
                make(t)["ov"][1]().wait_recv()

            start(make, t, ["relay"])

        sides = [(side, kv) for kv in range(2) for side in ("left", "right")]
        outs = [("out", 0), ("out", 1)]

        def forward(t):
            arrived(first, t, ["left", "right"])
            start(second, t, ["in", *outs])
            arrived(first, t, ["o", "ok"])
            start(second, t, sides[:2])
            arrived_values(first, t)
            start(second, t, sides[2:])

        sign = 1 - 2 * core
        bias = []
        for b in range(SECTORS):
            codes = []
            for s in range(SAMPLES):
                block = blocks[0, b, s]
                band = block // sector_total
                sector = block % sector_total
                column = (sector - (SECTORS * j + b) + 1 + sector_total) % sector_total
                codes.append((1 + sign * (band - i)) * 3 + column)
            row = []
            for o in range(9):
                listed = codes[0] == o
                for code in codes[1:]:
                    listed = listed | (code == o)
                row.append(jnp.where(listed, 0.0, HIDE).astype(jnp.float32))
            bias.append(row)

        head = lax.broadcasted_iota(jnp.int32, (CELLS, CH), 1) // HEAD_DIM
        on = [jnp.where(head == h, 1.0, 0.0).astype(jnp.float32) for h in range(PER)]
        on_low = [o.astype(jnp.bfloat16) for o in on]

        def spread(x):
            return jnp.concatenate([x * m for m in on_low], axis=0)

        def gathered(x):
            total = x[0:CELLS] * on[0]
            for h in range(1, PER):
                total = total + x[h * CELLS : (h + 1) * CELLS] * on[h]
            return total

        def compute(t, n):
            u = t * N + n
            scale = HEAD_DIM ** -0.5
            grads = ([], [])
            for b in range(SECTORS):
                qbd = spread(qs[u, b])
                dbd = spread(dos[u, b])
                keys = jnp.concatenate([ext[t, r, c, 0, n] for r in range(3) for c in SEEN[b]], axis=0)
                values = jnp.concatenate([ext[t, r, c, 1, n] for r in range(3) for c in SEEN[b]], axis=0)
                scores = dot(keys, qbd, 1, 1)
                scores = jnp.concatenate(
                    [scores[o * CELLS : (o + 1) * CELLS] + bias[b][o] for o in range(9)], axis=0
                )
                highest = jnp.max(scores, axis=0, keepdims=True)
                raised = jnp.exp((scores - highest) * scale)
                weights = raised * (1.0 / jnp.sum(raised, axis=0, keepdims=True))
                low = weights.astype(jnp.bfloat16)
                pressure = dot(values, dbd, 1, 1)
                inner = jnp.sum(weights * pressure, axis=0, keepdims=True)
                score_grad = (weights * (pressure - inner) * scale).astype(jnp.bfloat16)
                att_s[u, b] = gathered(dot(low, values, 0, 0)).astype(jnp.bfloat16)
                gq_s[u, b] = gathered(dot(score_grad, keys, 0, 0)).astype(jnp.bfloat16)
                grads[0].append(dot(score_grad, qbd, 1, 0).reshape(3, 3, CELLS, CH))
                grads[1].append(dot(low, dbd, 1, 0).reshape(3, 3, CELLS, CH))
            for kv in range(2):
                g0, g1 = grads[kv]
                for r in range(3):
                    edges = (g0[r, 0], g1[r, 2])
                    middle = (g0[r, 1] + g1[r, 0], g0[r, 2] + g1[r, 1])
                    for side in range(2):
                        if r == INNER:
                            s_in[t, side, kv, n] = edges[side].astype(jnp.bfloat16)
                            s_in[t, 2 + side, kv, n] = middle[side].astype(jnp.bfloat16)
                        elif r == OUTER:
                            s_oc[t, side, kv, n] = edges[side].astype(jnp.bfloat16)
                            g_out[u, side, kv] = middle[side]
                        else:
                            g_halo[u, side, kv] = edges[side]
                            g_own[u, side, kv] = middle[side]

        def middle(t):
            arrived(third, t, ["in", *outs])

            @pl.loop(0, N)
            def _(n):
                for side in range(2):
                    total = g_halo[t * N + n, side] + r_in[t, side, :, n].astype(jnp.float32)
                    s_halo[t, side, :, n] = (total + r_yc[t, side, :, n].astype(jnp.float32)).astype(jnp.bfloat16)

            start(fourth, t, ["left", "right"])
            arrived(third, t, sides)

            @pl.loop(0, N)
            def _(n):
                for side in range(2):
                    total = g_out[t * N + n, side] + r_oc[t, 1 - side, :, n].astype(jnp.float32)
                    s_out[t, side, :, n] = total.astype(jnp.bfloat16)

            start(fourth, t, ["o", "ok", "ov"])

        def finish(t):
            arrived(fourth, t, ["o", "ok"])
            arrived_values(fourth, t)
            arrived(fourth, t, ["left", "right"])

            @pl.loop(0, N)
            def _(n):
                for side in range(2):
                    total = (
                        g_own[t * N + n, side]
                        + r_in[t, 2 + side, :, n].astype(jnp.float32)
                        + jnp.where(inside, r_out[t, side, :, n].astype(jnp.float32), 0.0)
                        + r_halo[t, 1 - side, :, n].astype(jnp.float32)
                    )
                    gkv_s[t * N + n, side] = total.astype(jnp.bfloat16)

            for u in range(t * N, t * N + N):
                for copy in stores(u)[2:]:
                    copy.start()

        for u in range(STEPS):
            for copy in loads(u)[:2]:
                copy.start()
        for u in range(STEPS):
            for copy in loads(u)[2:]:
                copy.start()

        def greet(device):
            pl.semaphore_signal(barrier, inc=1, device_id=device, device_id_type=pl.DeviceIdType.MESH)

        barrier = pltpu.get_barrier_semaphore()
        for device in (to_lat(partner), to_lon(left), to_lon(right), to_lat(values_to)):
            greet(device)

        @pl.when(edge)
        def _():
            greet(to_lat(values_from))

        @pl.when(seam)
        def _():
            greet(to_lat(values_from))
            greet(to_lat(outer))

        def clear(when, ref, *at):
            @pl.when(when)
            def _():
                @pl.loop(0, NC)
                def _(t):
                    ref[(t, *at)] = jnp.zeros(ref.shape[1 + len(at) :], ref.dtype)

        for place in range(4):
            clear(edge, ext, OUTER, place, 0)
        for side in range(2):
            clear(edge, ext, OUTER, side, 1)
            clear(edge, r_out, side, 0)
            for kv in range(2):
                clear(jnp.logical_not(by_lon[kv]), r_oc, side, kv)
                clear(jnp.logical_not(by_lat[kv]), r_yc, side, kv)
        for u in range(STEPS):
            for copy in loads(u)[:2]:
                copy.wait()

        for when, peers in ((plain, 4), (edge, 5), (seam, 6)):

            @pl.when(when)
            def _():
                pl.semaphore_wait(barrier, peers)

        for t in range(NC):
            start(first, t, ["left", "right", "o", "ok", "ov", "in"])
        forward(0)
        for u in range(STEPS):
            for copy in loads(u)[2:]:
                copy.wait()
        for t in range(NC):
            if t + 1 < NC:
                forward(t + 1)
            arrived(first, t, ["in"])
            arrived(second, t, ["in", *sides, *outs])

            @pl.loop(0, N)
            def _(n):
                compute(t, n)

            start(third, t, ["in", *sides, *outs])
            for u in range(t * N, t * N + N):
                for copy in stores(u)[:2]:
                    copy.start()
            if t >= 1:
                middle(t - 1)
            if t >= 2:
                finish(t - 2)
        middle(NC - 1)
        if NC > 1:
            finish(NC - 2)
        finish(NC - 1)
        for t in range(NC):
            for make in (first, second, third, fourth):
                each(make, t, list(make(t)), lambda copy: copy.wait_send())
        for u in range(STEPS):
            for copy in stores(u):
                copy.wait()

    return kernel


def hand_over(*refs):
    copies = [pltpu.make_async_copy(refs[k], refs[3 + k], refs[6].at[k]) for k in range(3)]
    for copy in copies:
        copy.start()
    for copy in copies:
        copy.wait()


def solution(mesh):
    kernel = make_kernel(mesh.shape["lat"], mesh.shape["lon"])
    low, full = jnp.bfloat16, jnp.float32
    pair = (STEPS, 2, CELLS, CH)
    quad = (STEPS, 2, 2, CELLS, CH)
    sent = (NC, 2, 2, N, CELLS, CH)
    wide = (NC, 4, 2, N, CELLS, CH)

    def body(queries, keys_values, cotangent, blocks):
        far = pl.BlockSpec(memory_space=pltpu.HBM)
        results = pl.pallas_call(
            kernel,
            out_shape=(
                jax.ShapeDtypeStruct(queries.shape, low),
                jax.ShapeDtypeStruct(queries.shape, low),
                jax.ShapeDtypeStruct(keys_values.shape, low),
            ),
            in_specs=[pl.BlockSpec(memory_space=pltpu.SMEM), far, far, far],
            out_specs=(far, far, far),
            scratch_shapes=[
                pltpu.VMEM((NC, 3, 4, 2, N, CELLS, CH), low),
                *[pltpu.VMEM(pair, low)] * 4,
                pltpu.VMEM(quad, low),
                *[pltpu.VMEM(quad, full)] * 3,
                pltpu.VMEM(sent, low),
                pltpu.VMEM(wide, low),
                *[pltpu.VMEM(sent, low)] * 4,
                pltpu.VMEM(wide, low),
                *[pltpu.VMEM(sent, low)] * 2,
                pltpu.SemaphoreType.DMA((NC, 23)),
                pltpu.SemaphoreType.DMA((NC, 23)),
                pltpu.SemaphoreType.DMA((STEPS, 4)),
                pltpu.SemaphoreType.DMA((STEPS, 4)),
            ],
            compiler_params=pltpu.CompilerParams(
                collective_id=0, has_side_effects=True, vmem_limit_bytes=62 * 1024 * 1024
            ),
            cost_estimate=pl.CostEstimate(flops=4_000_000_000, bytes_accessed=4_000_000, transcendentals=1_200_000),
        )(blocks, queries, keys_values, cotangent)
        return pl.pallas_call(
            hand_over,
            out_shape=tuple(jax.ShapeDtypeStruct(r.shape, r.dtype) for r in results),
            in_specs=[pl.BlockSpec(memory_space=pltpu.VMEM)] * 3,
            out_specs=(far,) * 3,
            scratch_shapes=[pltpu.SemaphoreType.DMA((3,))],
        )(*results)

    placed = (
        P("lat", "lon", None, None),
        P(None, "lat", "lon", None, None),
        P("lat", "lon", None, None),
        P("lat", "lon", None),
    )
    return jax.shard_map(
        body,
        mesh=mesh,
        in_specs=placed,
        out_specs=(placed[0], placed[0], placed[1]),
        check_vma=False,
    )
```

```python
import jax
import jax.numpy as jnp
from jax import lax
from jax.experimental import pallas as pl
from jax.experimental.pallas import tpu as pltpu
from jax.sharding import PartitionSpec as P

HEAD_DIM = 64
CELLS = 64
D = 1024
CH = 256
STEPS = D // CH
PER = CH // HEAD_DIM
NC = 2
N = STEPS // NC
SECTORS = 2
SAMPLES = 6
OUTER, OWN, INNER = 0, 1, 2


def dot(a, b, ca, cb):
    return lax.dot_general(a, b, (((ca,), (cb,)), ((), ())), preferred_element_type=jnp.float32)


def make_kernel(n_lat, n_lon):
    sector_total = n_lon * SECTORS

    def kernel(
        blocks, q_hbm, kv_hbm, do_hbm, att_hbm, gq_hbm, gkv_hbm,
        ext, qs, dos, att_s, gq_s, gkv_s, g_own, g_out, g_halo,
        s_oc, s_in, s_out, s_halo, r_oc, r_yc, r_in, r_out, r_halo,
        near, grads, send_sem, recv_sem, load_sem, store_sem,
    ):
        i = lax.axis_index("lat")
        j = lax.axis_index("lon")
        core = lax.rem(i, 2)
        partner = i + 1 - 2 * core
        half = n_lat // 2
        edge = (i == 0) | (i == n_lat - 1)
        seam = (i == half - 1) | (i == half)
        inside = jnp.logical_not(edge)
        plain = inside & jnp.logical_not(seam)
        beside = plain & (i >= half - 3) & (i <= half + 2)
        by_lon = (inside & jnp.logical_not(beside), seam)
        by_lat = (beside, plain)
        outer = jnp.where(edge, partner, i + 2 * core - 1)
        values_to = jnp.where(i == half - 1, 0, jnp.where(i == half, n_lat - 1, outer))
        values_to = jnp.where(i == 0, half, jnp.where(i == n_lat - 1, half - 1, values_to))
        values_from = jnp.where(i == half - 1, n_lat - 1, jnp.where(i == half, 0, outer))
        values_from = jnp.where(i == 0, half - 1, jnp.where(i == n_lat - 1, half, values_from))
        left = lax.rem(j + n_lon - 1, n_lon)
        right = lax.rem(j + 1, n_lon)

        def cols(u):
            return pl.ds(u * CH, CH)

        def loads(u):
            return [
                pltpu.make_async_copy(kv_hbm.at[0, 0, :, :, cols(u)], ext.at[u // N, OWN, 2:4, 0, u % N], load_sem.at[u, 0]),
                pltpu.make_async_copy(kv_hbm.at[1, 0, :, :, cols(u)], ext.at[u // N, OWN, 2:4, 1, u % N], load_sem.at[u, 1]),
                pltpu.make_async_copy(q_hbm.at[0, :, :, cols(u)], qs.at[u], load_sem.at[u, 2]),
                pltpu.make_async_copy(do_hbm.at[0, :, :, cols(u)], dos.at[u], load_sem.at[u, 3]),
            ]

        def stores(u):
            return [
                pltpu.make_async_copy(att_s.at[u], att_hbm.at[0, :, :, cols(u)], store_sem.at[u, 0]),
                pltpu.make_async_copy(gq_s.at[u], gq_hbm.at[0, :, :, cols(u)], store_sem.at[u, 1]),
                pltpu.make_async_copy(gkv_s.at[u, :, 0], gkv_hbm.at[0, 0, :, :, cols(u)], store_sem.at[u, 2]),
                pltpu.make_async_copy(gkv_s.at[u, :, 1], gkv_hbm.at[1, 0, :, :, cols(u)], store_sem.at[u, 3]),
            ]

        def remote(t, kind, src, dst, device, when=None):
            def make():
                return pltpu.make_async_remote_copy(
                    src_ref=src, dst_ref=dst, send_sem=send_sem.at[t, kind], recv_sem=recv_sem.at[t, kind],
                    device_id=device, device_id_type=pl.DeviceIdType.MESH,
                )

            return when, make

        def to_lat(where):
            return (where, j)

        def to_lon(where):
            return (i, where)

        def owners(t, kind, src, dst):
            return {
                "o": remote(t, kind, src, dst, to_lat(outer), plain),
                "ok": remote(t, kind, src.at[:, 0], dst.at[:, 0], to_lat(outer), seam),
                "ov": remote(t, kind + 1, src.at[:, 1], dst.at[:, 1], to_lat(values_to), seam),
                "relay": remote(t, kind + 1, dst.at[:, 1], dst.at[:, 1], to_lat(values_to), edge),
            }

        def first(t):
            own = ext.at[t, OWN]
            return {
                **owners(t, 0, own.at[2:4], ext.at[t, OUTER, 2:4]),
                "left": remote(t, 2, own.at[2], own.at[1], to_lon(left)),
                "right": remote(t, 3, own.at[3], own.at[0], to_lon(right)),
                "in": remote(t, 4, own.at[2:4], ext.at[t, INNER, 2:4], to_lat(partner)),
            }

        def second(t):
            home, far, across = ext.at[t, OWN], ext.at[t, OUTER], ext.at[t, INNER]
            found = {"in": remote(t, 5, home.at[0:2], across.at[0:2], to_lat(partner))}
            for kv in range(2):
                found["left", kv] = remote(t, 6 + kv, far.at[2, kv], far.at[1, kv], to_lon(left), by_lon[kv])
                found["right", kv] = remote(t, 8 + kv, far.at[3, kv], far.at[0, kv], to_lon(right), by_lon[kv])
                found["out", kv] = remote(t, 10 + kv, home.at[0:2, kv], far.at[0:2, kv], to_lat(outer), by_lat[kv])
            return found

        def third(t):
            found = {"in": remote(t, 12, s_in.at[t], r_in.at[t], to_lat(partner))}
            for kv in range(2):
                found["left", kv] = remote(t, 13 + kv, s_oc.at[t, 0, kv], r_oc.at[t, 0, kv], to_lon(left), by_lon[kv])
                found["right", kv] = remote(t, 15 + kv, s_oc.at[t, 1, kv], r_oc.at[t, 1, kv], to_lon(right), by_lon[kv])
                found["out", kv] = remote(t, 17 + kv, s_oc.at[t, :, kv], r_yc.at[t, :, kv], to_lat(outer), by_lat[kv])
            return found

        def fourth(t):
            return {
                **owners(t, 19, s_out.at[t], r_out.at[t]),
                "left": remote(t, 21, s_halo.at[t, 0], r_halo.at[t, 0], to_lon(left)),
                "right": remote(t, 22, s_halo.at[t, 1], r_halo.at[t, 1], to_lon(right)),
            }

        def each(make, t, names, act):
            copies = [make(t)[name] for name in names]
            while copies:
                when = copies[0][0]
                same = [copy for copy in copies if copy[0] is when]
                copies = [copy for copy in copies if copy[0] is not when]

                def run():
                    for _, copy in same:
                        act(copy())

                if when is None:
                    run()
                else:
                    pl.when(when)(run)

        def start(make, t, names):
            each(make, t, names, lambda copy: copy.start())

        def arrived(make, t, names):
            each(make, t, names, lambda copy: copy.wait_recv())

        def pass_on(make, t):
            @pl.when(edge)
            def _():
                make(t)["ov"][1]().wait_recv()
                make(t)["relay"][1]().start()

        def arrived_values(make, t):
            @pl.when(seam)
            def _():
                make(t)["ov"][1]().wait_recv()

        sides = [(side, kv) for kv in range(2) for side in ("left", "right")]
        outs = [("out", 0), ("out", 1)]

        def forward(t):
            arrived(first, t, ["left", "right"])
            start(second, t, ["in", *outs])
            arrived(first, t, ["o", "ok"])
            start(second, t, sides[:2])
            pass_on(first, t)
            arrived_values(first, t)
            start(second, t, sides[2:])

        sign = 1 - 2 * core
        listed, slot = [], []
        for b in range(SECTORS):
            codes, row = [], []
            for s in range(SAMPLES):
                block = blocks[0, b, s]
                band = block // sector_total
                sector = block % sector_total
                column = (sector - (SECTORS * j + b) + 1 + sector_total) % sector_total
                role = 1 + sign * (band - i)
                codes.append(role * 3 + column)
                place = jnp.where(column == 0, 0, column + 1) if b == 0 else jnp.where(column == 2, 1, column + 2)
                row.append(jnp.minimum(jnp.maximum(role * 4 + place, 0), 11))
            listed.append(row)
            row = []
            for o in range(9):
                found = SAMPLES
                for s in range(SAMPLES):
                    found = jnp.where(codes[s] == o, s, found)
                row.append(found)
            slot.append(row)
        for b in range(SECTORS):
            for kv in range(2):
                grads[b, kv, SAMPLES] = jnp.zeros((CELLS, CH), jnp.float32)

        head = lax.broadcasted_iota(jnp.int32, (CELLS, CH), 1) // HEAD_DIM
        on = [jnp.where(head == h, 1.0, 0.0).astype(jnp.float32) for h in range(PER)]
        on_low = [o.astype(jnp.bfloat16) for o in on]

        def spread(x):
            return jnp.concatenate([x * m for m in on_low], axis=0)

        def gathered(x):
            total = x[0:CELLS] * on[0]
            for h in range(1, PER):
                total = total + x[h * CELLS : (h + 1) * CELLS] * on[h]
            return total

        def compute(t, n):
            u = t * N + n
            scale = HEAD_DIM ** -0.5
            for r in range(3):
                for c in range(4):
                    near[r * 4 + c] = ext[t, r, c, :, n]
            for b in range(SECTORS):
                qbd = spread(qs[u, b])
                dbd = spread(dos[u, b])
                keys = jnp.concatenate([near[block, 0] for block in listed[b]], axis=0)
                values = jnp.concatenate([near[block, 1] for block in listed[b]], axis=0)
                scores = dot(keys, qbd, 1, 1)
                highest = jnp.max(scores, axis=0, keepdims=True)
                raised = jnp.exp((scores - highest) * scale)
                weights = raised * (1.0 / jnp.sum(raised, axis=0, keepdims=True))
                low = weights.astype(jnp.bfloat16)
                pressure = dot(values, dbd, 1, 1)
                inner = jnp.sum(weights * pressure, axis=0, keepdims=True)
                score_grad = (weights * (pressure - inner) * scale).astype(jnp.bfloat16)
                att_s[u, b] = gathered(dot(low, values, 0, 0)).astype(jnp.bfloat16)
                gq_s[u, b] = gathered(dot(score_grad, keys, 0, 0)).astype(jnp.bfloat16)
                for kv, grad in enumerate((dot(score_grad, qbd, 1, 0), dot(low, dbd, 1, 0))):
                    for s in range(SAMPLES):
                        grads[b, kv, s] = grad[s * CELLS : (s + 1) * CELLS]
            for kv in range(2):
                for r in range(3):
                    g0, g1 = [[grads[b, kv, slot[b][3 * r + c]] for c in range(3)] for b in range(SECTORS)]
                    edges = (g0[0], g1[2])
                    middle = (g0[1] + g1[0], g0[2] + g1[1])
                    for side in range(2):
                        if r == INNER:
                            s_in[t, side, kv, n] = edges[side].astype(jnp.bfloat16)
                            s_in[t, 2 + side, kv, n] = middle[side].astype(jnp.bfloat16)
                        elif r == OUTER:
                            s_oc[t, side, kv, n] = edges[side].astype(jnp.bfloat16)
                            g_out[u, side, kv] = middle[side]
                        else:
                            g_halo[u, side, kv] = edges[side]
                            g_own[u, side, kv] = middle[side]

        def middle(t):
            arrived(third, t, ["in", *outs])

            @pl.loop(0, N)
            def _(n):
                for side in range(2):
                    total = g_halo[t * N + n, side] + r_in[t, side, :, n].astype(jnp.float32)
                    s_halo[t, side, :, n] = (total + r_yc[t, side, :, n].astype(jnp.float32)).astype(jnp.bfloat16)

            start(fourth, t, ["left", "right"])
            arrived(third, t, sides)

            @pl.loop(0, N)
            def _(n):
                for side in range(2):
                    total = g_out[t * N + n, side] + r_oc[t, 1 - side, :, n].astype(jnp.float32)
                    s_out[t, side, :, n] = total.astype(jnp.bfloat16)

            start(fourth, t, ["o", "ok", "ov"])

        def finish(t):
            arrived(fourth, t, ["o", "ok"])
            arrived_values(fourth, t)
            arrived(fourth, t, ["left", "right"])

            @pl.loop(0, N)
            def _(n):
                for side in range(2):
                    total = (
                        g_own[t * N + n, side]
                        + r_in[t, 2 + side, :, n].astype(jnp.float32)
                        + jnp.where(inside, r_out[t, side, :, n].astype(jnp.float32), 0.0)
                        + r_halo[t, 1 - side, :, n].astype(jnp.float32)
                    )
                    gkv_s[t * N + n, side] = total.astype(jnp.bfloat16)

            for u in range(t * N, t * N + N):
                for copy in stores(u)[2:]:
                    copy.start()

        for u in range(STEPS):
            for copy in loads(u)[:2]:
                copy.start()
        for u in range(STEPS):
            for copy in loads(u)[2:]:
                copy.start()

        def greet(device):
            pl.semaphore_signal(barrier, inc=1, device_id=device, device_id_type=pl.DeviceIdType.MESH)

        barrier = pltpu.get_barrier_semaphore()
        for device in (to_lat(partner), to_lon(left), to_lon(right), to_lat(values_to)):
            greet(device)

        @pl.when(edge)
        def _():
            greet(to_lat(values_from))

        @pl.when(seam)
        def _():
            greet(to_lat(values_from))
            greet(to_lat(outer))

        def clear(when, ref, *at):
            @pl.when(when)
            def _():
                @pl.loop(0, NC)
                def _(t):
                    ref[(t, *at)] = jnp.zeros(ref.shape[1 + len(at) :], ref.dtype)

        for place in range(4):
            clear(edge, ext, OUTER, place, 0)
        for side in range(2):
            clear(edge, ext, OUTER, side, 1)
            clear(edge, r_out, side, 0)
            for kv in range(2):
                clear(jnp.logical_not(by_lon[kv]), r_oc, side, kv)
                clear(jnp.logical_not(by_lat[kv]), r_yc, side, kv)
        for u in range(STEPS):
            for copy in loads(u)[:2]:
                copy.wait()

        for when, peers in ((plain, 4), (edge, 5), (seam, 6)):

            @pl.when(when)
            def _():
                pl.semaphore_wait(barrier, peers)

        def send(t):
            start(first, t, ["left", "right", "o", "ok", "ov", "in"])

        def work(t):
            arrived(first, t, ["in"])
            arrived(second, t, ["in", *sides, *outs])
            if t == 0:
                for u in range(STEPS):
                    for copy in loads(u)[2:]:
                        copy.wait()

            @pl.loop(0, N)
            def _(n):
                compute(t, n)

            start(third, t, ["in", *sides, *outs])
            for u in range(t * N, t * N + N):
                for copy in stores(u)[:2]:
                    copy.start()

        send(0)
        send(1)
        forward(0)
        forward(1)
        work(0)
        work(1)
        middle(0)
        pass_on(fourth, 0)
        middle(1)
        pass_on(fourth, 1)
        finish(0)
        finish(1)
        for t in range(NC):
            for make in (first, second, third, fourth):
                each(make, t, list(make(t)), lambda copy: copy.wait_send())
        for u in range(STEPS):
            for copy in stores(u):
                copy.wait()

    return kernel


def hand_over(*refs):
    sources, results, held, sem = refs[:3], refs[3:6], refs[6:9], refs[9]
    loads = [pltpu.make_async_copy(sources[k], held[k], sem.at[0, k]) for k in range(3)]
    stores = [pltpu.make_async_copy(held[k], results[k], sem.at[1, k]) for k in range(3)]
    for copy in loads:
        copy.start()
    for load, store in zip(loads, stores):
        load.wait()
        store.start()
    for copy in stores:
        copy.wait()


def solution(mesh):
    kernel = make_kernel(mesh.shape["lat"], mesh.shape["lon"])
    low, full = jnp.bfloat16, jnp.float32
    pair = (STEPS, 2, CELLS, CH)
    quad = (STEPS, 2, 2, CELLS, CH)
    sent = (NC, 2, 2, N, CELLS, CH)
    wide = (NC, 4, 2, N, CELLS, CH)

    def body(queries, keys_values, cotangent, blocks):
        far = pl.BlockSpec(memory_space=pltpu.HBM)
        results = pl.pallas_call(
            kernel,
            out_shape=(
                jax.ShapeDtypeStruct(queries.shape, low),
                jax.ShapeDtypeStruct(queries.shape, low),
                jax.ShapeDtypeStruct(keys_values.shape, low),
            ),
            in_specs=[pl.BlockSpec(memory_space=pltpu.SMEM), far, far, far],
            out_specs=(far, far, far),
            scratch_shapes=[
                pltpu.VMEM((NC, 3, 4, 2, N, CELLS, CH), low),
                *[pltpu.VMEM(pair, low)] * 4,
                pltpu.VMEM(quad, low),
                *[pltpu.VMEM(quad, full)] * 3,
                pltpu.VMEM(sent, low),
                pltpu.VMEM(wide, low),
                *[pltpu.VMEM(sent, low)] * 4,
                pltpu.VMEM(wide, low),
                *[pltpu.VMEM(sent, low)] * 2,
                pltpu.VMEM((12, 2, CELLS, CH), low),
                pltpu.VMEM((SECTORS, 2, SAMPLES + 1, CELLS, CH), full),
                pltpu.SemaphoreType.DMA((NC, 23)),
                pltpu.SemaphoreType.DMA((NC, 23)),
                pltpu.SemaphoreType.DMA((STEPS, 4)),
                pltpu.SemaphoreType.DMA((STEPS, 4)),
            ],
            compiler_params=pltpu.CompilerParams(
                collective_id=0, has_side_effects=True, vmem_limit_bytes=62 * 1024 * 1024
            ),
            cost_estimate=pl.CostEstimate(flops=4_000_000_000, bytes_accessed=4_000_000, transcendentals=1_200_000),
        )(blocks, queries, keys_values, cotangent)
        return pl.pallas_call(
            hand_over,
            out_shape=tuple(jax.ShapeDtypeStruct(r.shape, r.dtype) for r in results),
            in_specs=[far] * 3,
            out_specs=(far,) * 3,
            scratch_shapes=[*[pltpu.VMEM(r.shape, r.dtype) for r in results], pltpu.SemaphoreType.DMA((2, 3))],
            compiler_params=pltpu.CompilerParams(vmem_limit_bytes=62 * 1024 * 1024),
        )(*results)

    placed = (
        P("lat", "lon", None, None),
        P(None, "lat", "lon", None, None),
        P("lat", "lon", None, None),
        P("lat", "lon", None),
    )
    return jax.shard_map(
        body,
        mesh=mesh,
        in_specs=placed,
        out_specs=(placed[0], placed[0], placed[1]),
        check_vma=False,
    )
```

```python
import jax
import jax.numpy as jnp
from jax import lax
from jax.experimental import pallas as pl
from jax.experimental.pallas import tpu as pltpu
from jax.sharding import PartitionSpec as P

HEAD_DIM = 64
CELLS = 64
D = 1024
CH = 256
STEPS = D // CH
PER = CH // HEAD_DIM
NC = 2
N = STEPS // NC
SECTORS = 2
SAMPLES = 6
OUTER, OWN, INNER = 0, 1, 2


def dot(a, b, ca, cb):
    return lax.dot_general(a, b, (((ca,), (cb,)), ((), ())), preferred_element_type=jnp.float32)


def make_kernel(n_lat, n_lon):
    sector_total = n_lon * SECTORS

    def kernel(
        blocks, q_hbm, kv_hbm, do_hbm, att_hbm, gq_hbm, gkv_hbm,
        ext, qs, dos, att_s, gq_s, gkv_s, g_own, g_out, g_halo,
        s_oc, s_in, s_out, s_halo, r_oc, r_yc, r_in, r_out, r_halo,
        near, grads, send_sem, recv_sem, load_sem, store_sem,
    ):
        i = lax.axis_index("lat")
        j = lax.axis_index("lon")
        core = lax.rem(i, 2)
        partner = i + 1 - 2 * core
        half = n_lat // 2
        edge = (i == 0) | (i == n_lat - 1)
        seam = (i == half - 1) | (i == half)
        inside = jnp.logical_not(edge)
        plain = inside & jnp.logical_not(seam)
        beside = plain & (i >= half - 3) & (i <= half + 2)
        by_lon = (inside & jnp.logical_not(beside), seam)
        by_lat = (beside, plain)
        outer = jnp.where(edge, partner, i + 2 * core - 1)
        values_to = jnp.where(i == half - 1, 0, jnp.where(i == half, n_lat - 1, outer))
        values_to = jnp.where(i == 0, half, jnp.where(i == n_lat - 1, half - 1, values_to))
        values_from = jnp.where(i == half - 1, n_lat - 1, jnp.where(i == half, 0, outer))
        values_from = jnp.where(i == 0, half - 1, jnp.where(i == n_lat - 1, half, values_from))
        left = lax.rem(j + n_lon - 1, n_lon)
        right = lax.rem(j + 1, n_lon)

        def to_lat(where):
            return (where, j)

        def to_lon(where):
            return (i, where)

        def greet(device):
            pl.semaphore_signal(barrier, inc=1, device_id=device, device_id_type=pl.DeviceIdType.MESH)

        barrier = pltpu.get_barrier_semaphore()
        for device in (to_lat(partner), to_lon(left), to_lon(right), to_lat(values_to)):
            greet(device)

        @pl.when(edge)
        def _():
            greet(to_lat(values_from))

        @pl.when(seam)
        def _():
            greet(to_lat(values_from))
            greet(to_lat(outer))

        def cols(u):
            return pl.ds(u * CH, CH)

        def loads(u):
            return [
                pltpu.make_async_copy(kv_hbm.at[0, 0, :, :, cols(u)], ext.at[u // N, OWN, 2:4, 0, u % N], load_sem.at[u, 0]),
                pltpu.make_async_copy(kv_hbm.at[1, 0, :, :, cols(u)], ext.at[u // N, OWN, 2:4, 1, u % N], load_sem.at[u, 1]),
                pltpu.make_async_copy(q_hbm.at[0, :, :, cols(u)], qs.at[u], load_sem.at[u, 2]),
                pltpu.make_async_copy(do_hbm.at[0, :, :, cols(u)], dos.at[u], load_sem.at[u, 3]),
            ]

        def stores(u):
            return [
                pltpu.make_async_copy(att_s.at[u], att_hbm.at[0, :, :, cols(u)], store_sem.at[u, 0]),
                pltpu.make_async_copy(gq_s.at[u], gq_hbm.at[0, :, :, cols(u)], store_sem.at[u, 1]),
                pltpu.make_async_copy(gkv_s.at[u, :, 0], gkv_hbm.at[0, 0, :, :, cols(u)], store_sem.at[u, 2]),
                pltpu.make_async_copy(gkv_s.at[u, :, 1], gkv_hbm.at[1, 0, :, :, cols(u)], store_sem.at[u, 3]),
            ]

        for u in range(STEPS):
            for copy in loads(u)[:2]:
                copy.start()
        for u in range(STEPS):
            for copy in loads(u)[2:]:
                copy.start()

        def remote(t, kind, src, dst, device, when=None):
            def make():
                return pltpu.make_async_remote_copy(
                    src_ref=src, dst_ref=dst, send_sem=send_sem.at[t, kind], recv_sem=recv_sem.at[t, kind],
                    device_id=device, device_id_type=pl.DeviceIdType.MESH,
                )

            return when, make

        def owners(t, kind, src, dst):
            return {
                "o": remote(t, kind, src, dst, to_lat(outer), plain),
                "ok": remote(t, kind, src.at[:, 0], dst.at[:, 0], to_lat(outer), seam),
                "ov": remote(t, kind + 1, src.at[:, 1], dst.at[:, 1], to_lat(values_to), seam),
                "relay": remote(t, kind + 1, dst.at[:, 1], dst.at[:, 1], to_lat(values_to), edge),
            }

        def first(t):
            own = ext.at[t, OWN]
            return {
                **owners(t, 0, own.at[2:4], ext.at[t, OUTER, 2:4]),
                "left": remote(t, 2, own.at[2], own.at[1], to_lon(left)),
                "right": remote(t, 3, own.at[3], own.at[0], to_lon(right)),
                "in": remote(t, 4, own.at[2:4], ext.at[t, INNER, 2:4], to_lat(partner)),
            }

        def second(t):
            home, far, across = ext.at[t, OWN], ext.at[t, OUTER], ext.at[t, INNER]
            found = {"in": remote(t, 5, home.at[0:2], across.at[0:2], to_lat(partner))}
            for kv in range(2):
                found["left", kv] = remote(t, 6 + kv, far.at[2, kv], far.at[1, kv], to_lon(left), by_lon[kv])
                found["right", kv] = remote(t, 8 + kv, far.at[3, kv], far.at[0, kv], to_lon(right), by_lon[kv])
                found["out", kv] = remote(t, 10 + kv, home.at[0:2, kv], far.at[0:2, kv], to_lat(outer), by_lat[kv])
            return found

        def third(t):
            found = {"in": remote(t, 12, s_in.at[t], r_in.at[t], to_lat(partner))}
            for kv in range(2):
                found["left", kv] = remote(t, 13 + kv, s_oc.at[t, 0, kv], r_oc.at[t, 0, kv], to_lon(left), by_lon[kv])
                found["right", kv] = remote(t, 15 + kv, s_oc.at[t, 1, kv], r_oc.at[t, 1, kv], to_lon(right), by_lon[kv])
                found["out", kv] = remote(t, 17 + kv, s_oc.at[t, :, kv], r_yc.at[t, :, kv], to_lat(outer), by_lat[kv])
            return found

        def fourth(t):
            return {
                **owners(t, 19, s_out.at[t], r_out.at[t]),
                "left": remote(t, 21, s_halo.at[t, 0], r_halo.at[t, 0], to_lon(left)),
                "right": remote(t, 22, s_halo.at[t, 1], r_halo.at[t, 1], to_lon(right)),
            }

        def each(make, t, names, act):
            copies = [make(t)[name] for name in names]
            while copies:
                when = copies[0][0]
                same = [copy for copy in copies if copy[0] is when]
                copies = [copy for copy in copies if copy[0] is not when]

                def run():
                    for _, copy in same:
                        act(copy())

                if when is None:
                    run()
                else:
                    pl.when(when)(run)

        def start(make, t, names):
            each(make, t, names, lambda copy: copy.start())

        def arrived(make, t, names):
            each(make, t, names, lambda copy: copy.wait_recv())

        def pass_on(make, t):
            @pl.when(edge)
            def _():
                make(t)["ov"][1]().wait_recv()
                make(t)["relay"][1]().start()

        def arrived_values(make, t):
            @pl.when(seam)
            def _():
                make(t)["ov"][1]().wait_recv()

        sides = [(side, kv) for kv in range(2) for side in ("left", "right")]
        outs = [("out", 0), ("out", 1)]

        def forward(t):
            arrived(first, t, ["left", "right"])
            start(second, t, ["in", *outs])
            arrived(first, t, ["o", "ok"])
            start(second, t, sides[:2])
            pass_on(first, t)
            arrived_values(first, t)
            start(second, t, sides[2:])

        sign = 1 - 2 * core
        listed, slot = [], []
        for b in range(SECTORS):
            codes, row = [], []
            for s in range(SAMPLES):
                block = blocks[0, b, s]
                band = block // sector_total
                sector = block % sector_total
                column = (sector - (SECTORS * j + b) + 1 + sector_total) % sector_total
                role = 1 + sign * (band - i)
                codes.append(role * 3 + column)
                place = jnp.where(column == 0, 0, column + 1) if b == 0 else jnp.where(column == 2, 1, column + 2)
                row.append(jnp.minimum(jnp.maximum(role * 4 + place, 0), 11))
            listed.append(row)
            row = []
            for o in range(9):
                found = SAMPLES
                for s in range(SAMPLES):
                    found = jnp.where(codes[s] == o, s, found)
                row.append(found)
            slot.append(row)
        for b in range(SECTORS):
            for kv in range(2):
                grads[b, kv, SAMPLES] = jnp.zeros((CELLS, CH), jnp.float32)

        head = lax.broadcasted_iota(jnp.int32, (CELLS, CH), 1) // HEAD_DIM
        on = [jnp.where(head == h, 1.0, 0.0).astype(jnp.float32) for h in range(PER)]
        on_low = [o.astype(jnp.bfloat16) for o in on]

        def spread(x):
            return jnp.concatenate([x * m for m in on_low], axis=0)

        def gathered(x):
            total = x[0:CELLS] * on[0]
            for h in range(1, PER):
                total = total + x[h * CELLS : (h + 1) * CELLS] * on[h]
            return total

        def compute(t, n):
            u = t * N + n
            scale = HEAD_DIM ** -0.5
            for r in range(3):
                for c in range(4):
                    near[r * 4 + c] = ext[t, r, c, :, n]
            for b in range(SECTORS):
                qbd = spread(qs[u, b])
                dbd = spread(dos[u, b])
                keys = jnp.concatenate([near[block, 0] for block in listed[b]], axis=0)
                values = jnp.concatenate([near[block, 1] for block in listed[b]], axis=0)
                scores = dot(keys, qbd, 1, 1)
                highest = jnp.max(scores, axis=0, keepdims=True)
                raised = jnp.exp((scores - highest) * scale)
                weights = raised * (1.0 / jnp.sum(raised, axis=0, keepdims=True))
                low = weights.astype(jnp.bfloat16)
                pressure = dot(values, dbd, 1, 1)
                inner = jnp.sum(weights * pressure, axis=0, keepdims=True)
                score_grad = (weights * (pressure - inner) * scale).astype(jnp.bfloat16)
                att_s[u, b] = gathered(dot(low, values, 0, 0)).astype(jnp.bfloat16)
                gq_s[u, b] = gathered(dot(score_grad, keys, 0, 0)).astype(jnp.bfloat16)
                for kv, grad in enumerate((dot(score_grad, qbd, 1, 0), dot(low, dbd, 1, 0))):
                    for s in range(SAMPLES):
                        grads[b, kv, s] = grad[s * CELLS : (s + 1) * CELLS]
            for kv in range(2):
                for r in range(3):
                    g0, g1 = [[grads[b, kv, slot[b][3 * r + c]] for c in range(3)] for b in range(SECTORS)]
                    edges = (g0[0], g1[2])
                    middle = (g0[1] + g1[0], g0[2] + g1[1])
                    for side in range(2):
                        if r == INNER:
                            s_in[t, side, kv, n] = edges[side].astype(jnp.bfloat16)
                            s_in[t, 2 + side, kv, n] = middle[side].astype(jnp.bfloat16)
                        elif r == OUTER:
                            s_oc[t, side, kv, n] = edges[side].astype(jnp.bfloat16)
                            g_out[u, side, kv] = middle[side]
                        else:
                            g_halo[u, side, kv] = edges[side]
                            g_own[u, side, kv] = middle[side]

        def middle(t):
            arrived(third, t, ["in", *outs])

            @pl.loop(0, N)
            def _(n):
                for side in range(2):
                    total = g_halo[t * N + n, side] + r_in[t, side, :, n].astype(jnp.float32)
                    s_halo[t, side, :, n] = (total + r_yc[t, side, :, n].astype(jnp.float32)).astype(jnp.bfloat16)

            start(fourth, t, ["left", "right"])
            arrived(third, t, sides)

            @pl.loop(0, N)
            def _(n):
                for side in range(2):
                    total = g_out[t * N + n, side] + r_oc[t, 1 - side, :, n].astype(jnp.float32)
                    s_out[t, side, :, n] = total.astype(jnp.bfloat16)

            start(fourth, t, ["o", "ok", "ov"])

        def finish(t):
            arrived(fourth, t, ["o", "ok"])
            arrived_values(fourth, t)
            arrived(fourth, t, ["left", "right"])

            @pl.loop(0, N)
            def _(n):
                for side in range(2):
                    total = (
                        g_own[t * N + n, side]
                        + r_in[t, 2 + side, :, n].astype(jnp.float32)
                        + jnp.where(inside, r_out[t, side, :, n].astype(jnp.float32), 0.0)
                        + r_halo[t, 1 - side, :, n].astype(jnp.float32)
                    )
                    gkv_s[t * N + n, side] = total.astype(jnp.bfloat16)

            for u in range(t * N, t * N + N):
                for copy in stores(u)[2:]:
                    copy.start()

        def clear(when, ref, *at):
            @pl.when(when)
            def _():
                @pl.loop(0, NC)
                def _(t):
                    ref[(t, *at)] = jnp.zeros(ref.shape[1 + len(at) :], ref.dtype)

        for place in range(4):
            clear(edge, ext, OUTER, place, 0)
        for side in range(2):
            clear(edge, ext, OUTER, side, 1)
            clear(edge, r_out, side, 0)
            for kv in range(2):
                clear(jnp.logical_not(by_lon[kv]), r_oc, side, kv)
                clear(jnp.logical_not(by_lat[kv]), r_yc, side, kv)

        for when, peers in ((plain, 4), (edge, 5), (seam, 6)):

            @pl.when(when)
            def _():
                pl.semaphore_wait(barrier, peers)

        def send(t):
            for u in range(t * N, t * N + N):
                for copy in loads(u)[:2]:
                    copy.wait()
            start(first, t, ["left", "right", "o", "ok", "ov", "in"])

        def work(t):
            arrived(first, t, ["in"])
            arrived(second, t, ["in", *sides, *outs])
            if t == 0:
                for u in range(STEPS):
                    for copy in loads(u)[2:]:
                        copy.wait()

            @pl.loop(0, N)
            def _(n):
                compute(t, n)

            start(third, t, ["in", *sides, *outs])
            for u in range(t * N, t * N + N):
                for copy in stores(u)[:2]:
                    copy.start()

        send(0)
        send(1)
        forward(0)
        forward(1)
        work(0)
        work(1)
        middle(0)
        pass_on(fourth, 0)
        middle(1)
        pass_on(fourth, 1)
        finish(0)
        finish(1)
        for t in range(NC):
            for make in (first, second, third, fourth):
                each(make, t, list(make(t)), lambda copy: copy.wait_send())
        for u in range(STEPS):
            for copy in stores(u):
                copy.wait()

    return kernel


def hand_over(*refs):
    sources, results, held, sem = refs[:3], refs[3:6], refs[6:9], refs[9]
    loads = [pltpu.make_async_copy(sources[k], held[k], sem.at[0, k]) for k in range(3)]
    stores = [pltpu.make_async_copy(held[k], results[k], sem.at[1, k]) for k in range(3)]
    for copy in loads:
        copy.start()
    for load, store in zip(loads, stores):
        load.wait()
        store.start()
    for copy in stores:
        copy.wait()


def solution(mesh):
    kernel = make_kernel(mesh.shape["lat"], mesh.shape["lon"])
    low, full = jnp.bfloat16, jnp.float32
    pair = (STEPS, 2, CELLS, CH)
    quad = (STEPS, 2, 2, CELLS, CH)
    sent = (NC, 2, 2, N, CELLS, CH)
    wide = (NC, 4, 2, N, CELLS, CH)

    def body(queries, keys_values, cotangent, blocks):
        far = pl.BlockSpec(memory_space=pltpu.HBM)
        results = pl.pallas_call(
            kernel,
            out_shape=(
                jax.ShapeDtypeStruct(queries.shape, low),
                jax.ShapeDtypeStruct(queries.shape, low),
                jax.ShapeDtypeStruct(keys_values.shape, low),
            ),
            in_specs=[pl.BlockSpec(memory_space=pltpu.SMEM), far, far, far],
            out_specs=(far, far, far),
            scratch_shapes=[
                pltpu.VMEM((NC, 3, 4, 2, N, CELLS, CH), low),
                *[pltpu.VMEM(pair, low)] * 4,
                pltpu.VMEM(quad, low),
                *[pltpu.VMEM(quad, full)] * 3,
                pltpu.VMEM(sent, low),
                pltpu.VMEM(wide, low),
                *[pltpu.VMEM(sent, low)] * 4,
                pltpu.VMEM(wide, low),
                *[pltpu.VMEM(sent, low)] * 2,
                pltpu.VMEM((12, 2, CELLS, CH), low),
                pltpu.VMEM((SECTORS, 2, SAMPLES + 1, CELLS, CH), full),
                pltpu.SemaphoreType.DMA((NC, 23)),
                pltpu.SemaphoreType.DMA((NC, 23)),
                pltpu.SemaphoreType.DMA((STEPS, 4)),
                pltpu.SemaphoreType.DMA((STEPS, 4)),
            ],
            compiler_params=pltpu.CompilerParams(
                collective_id=0, has_side_effects=True, vmem_limit_bytes=62 * 1024 * 1024
            ),
            cost_estimate=pl.CostEstimate(flops=4_000_000_000, bytes_accessed=4_000_000, transcendentals=1_200_000),
        )(blocks, queries, keys_values, cotangent)
        return pl.pallas_call(
            hand_over,
            out_shape=tuple(jax.ShapeDtypeStruct(r.shape, r.dtype) for r in results),
            in_specs=[far] * 3,
            out_specs=(far,) * 3,
            scratch_shapes=[*[pltpu.VMEM(r.shape, r.dtype) for r in results], pltpu.SemaphoreType.DMA((2, 3))],
            compiler_params=pltpu.CompilerParams(vmem_limit_bytes=62 * 1024 * 1024),
        )(*results)

    placed = (
        P("lat", "lon", None, None),
        P(None, "lat", "lon", None, None),
        P("lat", "lon", None, None),
        P("lat", "lon", None),
    )
    return jax.shard_map(
        body,
        mesh=mesh,
        in_specs=placed,
        out_specs=(placed[0], placed[0], placed[1]),
        check_vma=False,
    )
```
